32 devices in a mesh: gx: 2 (over x), gy: 4 (over y, core), gz: 4 (over z).
Axes of the slice: x: 2, y: 2, z: 4, core: 2. Of those that a mesh axis runs over, the one named last changes fastest.
Arguments:
- charges: float32 [128, 1024, 256], P('gz', 'gy', 'gx'), may hold values from -8 to 8
- fine_taps: float32 [2, 3, 17], replicated, may hold values from 0.05 to 0.45
- coarse_taps: float32 [2, 3, 17], replicated, may hold values from 0.05 to 0.45
Outputs:
- potential: float32 [128, 1024, 256], P('gz', 'gy', 'gx')
The draws below stay inside these ranges and needn't reach their ends.
All inputs are finite; a program needn't handle non-finite values.
Results may differ from the reference program's by a relative error of at most 0.0003.
Values sent between devices are 32-bit elements; how exact they have to be, the bound alone decides.
A program may use at most 128 MiB of HBM per device.

```python
import math
import jax
import jax.numpy as jnp
from jax import lax

RADIUS = 8
TERMS = 2
TOPB = 16
TAPS = 17
NX = 256
NY = 1024
NZ = 128


def draw_charges(key, part):
    noise_key = jax.random.fold_in(key, 11)
    grid_shape = (NZ, NY, NX)
    return jax.random.truncated_normal(noise_key, -6.0, 6.0, grid_shape, jnp.float32)


def setup_inputs(seed: int = 0) -> dict:
    keys = jax.random.split(jax.random.key(seed), 4)
    return {
        "charges": draw_charges(jax.random.fold_in(keys[3], 71), 0),
        "fine_taps": jnp.clip(jax.random.uniform(keys[1], (TERMS, 3, TAPS), jnp.float32, 0.05, 0.45), 0.05, 0.45),
        "coarse_taps": jnp.clip(jax.random.uniform(keys[2], (TERMS, 3, TAPS), jnp.float32, 0.05, 0.45), 0.05, 0.45),
    }


def correlate(grid_field, tap_set):
    running = jnp.zeros(grid_field.shape, jnp.float32)
    for term_index in range(TERMS):
        current = grid_field
        for axis_pos, array_axis in ((0, 2), (1, 1), (2, 0)):
            summed = jnp.zeros(grid_field.shape, jnp.float32)
            for offset in range(-RADIUS, RADIUS + 1):
                summed = summed + tap_set[term_index, axis_pos, offset + RADIUS] * jnp.roll(current, -offset, axis=array_axis)
            current = summed
        running = running + current
    return running

def wrapped(anchor, target, period):
    distance = jnp.abs(anchor - target)
    return jnp.minimum(distance, period - distance).astype(jnp.float32)

def direct_top(top_grid):
    top_z, top_y, top_x = top_grid.shape
    cell_count = top_z * top_y * top_x
    flat_top = top_grid.reshape(-1)
    cell_ids = jnp.arange(cell_count, dtype=jnp.int32)
    z_cell = cell_ids // (top_y * top_x)
    y_cell = cell_ids // top_x % top_y
    x_cell = cell_ids % top_x
    row_block = math.gcd(cell_count, 512)

    def row_kernel(first_row):
        row_ids = first_row + jnp.arange(row_block, dtype=jnp.int32)
        dz = wrapped(row_ids[:, None] // (top_y * top_x), z_cell[None, :], top_z)
        dy = wrapped(row_ids[:, None] // top_x % top_y, y_cell[None, :], top_y)
        dx = wrapped(row_ids[:, None] % top_x, x_cell[None, :], top_x)
        kernel = 1.0 / (TOPB * TOPB * jnp.sqrt(1.0 + dz * dz + dy * dy + dx * dx))
        return jnp.dot(kernel, flat_top, precision=lax.Precision.HIGHEST)
    starts = jnp.arange(0, cell_count, row_block, dtype=jnp.int32)
    return lax.map(row_kernel, starts).reshape(top_grid.shape)

def expand(grid_field, factor):
    grid_field = jnp.repeat(grid_field, factor, axis=0)
    grid_field = jnp.repeat(grid_field, factor, axis=1)
    return jnp.repeat(grid_field, factor, axis=2)

def reference(charges, fine_taps, coarse_taps):
    fine_part = correlate(charges, fine_taps)
    coarse = charges.reshape(NZ // 2, 2, NY // 2, 2, NX // 2, 2).mean(axis=(1, 3, 5))
    coarse_part = correlate(coarse, coarse_taps)
    top_grid = coarse.reshape(NZ // (2 * TOPB), TOPB, NY // (2 * TOPB), TOPB, NX // (2 * TOPB), TOPB).sum(axis=(1, 3, 5))
    coarse_potential = coarse_part + expand(direct_top(top_grid), TOPB)
    return fine_part + expand(coarse_potential, 2)
```

```python
import functools

import jax
import jax.numpy as jnp
from jax import lax
from jax.experimental import pallas as pl
from jax.experimental.pallas import tpu as pltpu
from jax.sharding import PartitionSpec as P

RADIUS = 8
TOPB = 16
AXES = ("gz", "gy", "gx")
precise = lax.Precision.HIGHEST
f32, bf16 = jnp.float32, jnp.bfloat16


def shift(block, axis, by):
    n = lax.axis_size(axis)
    return lax.ppermute(block, axis, [(i, (i + by) % n) for i in range(n)])


def split(mat):
    high = lax.reduce_precision(mat, 8, 7)
    return high.astype(bf16), (mat - high).astype(bf16)


def split_in(val):
    high = val.astype(bf16)
    return high, (val - high.astype(f32)).astype(bf16)


def mm(a, b, dims=((1,), (0,))):
    return lax.dot_general(a, b, (dims, ((), ())), preferred_element_type=f32)


def mm3(a, b, dims=((1,), (0,))):
    return mm(a[0], b[0], dims) + mm(a[1], b[0], dims) + mm(a[0], b[1], dims)


def band(taps, length_in, length_out, repeat=1):
    spread = taps.shape[1]
    diff = (
        jnp.arange(length_in, dtype=jnp.int32)[:, None]
        - jnp.arange(length_out * repeat, dtype=jnp.int32)[None, :] // repeat
    )
    out = jnp.zeros((taps.shape[0],) + diff.shape, f32)
    for k in range(spread):
        out = jnp.where(diff[None] == k, taps[:, k, None, None], out)
    return out


def xy_kernel(planes, size_y, size_x, c_ref, ylo_ref, yhi_ref, xs_ref,
              bmh, bml, beh, bel, byh, byl, g_ref):
    ext_y = size_y + 2 * RADIUS
    rows = jnp.concatenate(
        [part for p in range(planes) for part in (ylo_ref[p], c_ref[p], yhi_ref[p])], axis=0
    )
    mid = mm3(split_in(rows), (bmh[...], bml[...]))
    parts = []
    for p in range(planes):
        edge = mm3(split_in(xs_ref[p]), (beh[...], bel[...]), ((0,), (0,)))
        parts.append(mid[p * ext_y:(p + 1) * ext_y] + edge)
    for t in range(2):
        right = jnp.concatenate([part[:, t * size_x:(t + 1) * size_x] for part in parts], axis=1)
        out = mm3((byh[t], byl[t]), split_in(right))
        for p in range(planes):
            g_ref[t, p] = out[:, p * size_x:(p + 1) * size_x]


def xy_pass(block, ylo, yhi, xs, mats):
    size_z, size_y, size_x = block.shape
    planes = 4
    whole = lambda a: pl.BlockSpec(a.shape, lambda i: (0,) * a.ndim)
    lead = lambda a: pl.BlockSpec((planes,) + a.shape[1:], lambda i: (i, 0, 0))
    return pl.pallas_call(
        functools.partial(xy_kernel, planes, size_y, size_x),
        grid=(size_z // planes,),
        in_specs=[lead(a) for a in (block, ylo, yhi, xs)] + [whole(m) for m in mats],
        out_specs=pl.BlockSpec((2, planes, size_y, size_x), lambda i: (0, i, 0, 0)),
        out_shape=jax.ShapeDtypeStruct((2, size_z, size_y, size_x), f32),
        compiler_params=pltpu.CompilerParams(vmem_limit_bytes=40 * 2**20),
        cost_estimate=pl.CostEstimate(
            flops=size_z * 2 * 600 * 10**6 // 10, bytes_accessed=3 * block.size * 4, transcendentals=0
        ),
    )(block, ylo, yhi, xs, *mats)


def z_own_kernel(size_z, groups, w_ref, g_ref, e_ref, o_ref):
    def body(r, carry):
        rows = pl.ds(pl.multiple_of(r * 8, 8), 8)
        acc = [e_ref[o // 2, rows, :] for o in range(size_z)]
        for t in range(2):
            for z in range(size_z):
                val = g_ref[t, z, rows, :]
                for o in range(max(0, z - RADIUS), min(size_z, z + RADIUS + 1)):
                    acc[o] = acc[o] + w_ref[t, z - o + RADIUS] * val
        for o in range(size_z):
            o_ref[o, rows, :] = acc[o]
        return carry

    lax.fori_loop(0, groups, body, 0)


def z_own(taps_z, g, expanded):
    _, size_z, size_y, size_x = g.shape
    blk = 32
    return pl.pallas_call(
        functools.partial(z_own_kernel, size_z, blk // 8),
        grid=(size_y // blk,),
        in_specs=[
            pl.BlockSpec(memory_space=pltpu.SMEM),
            pl.BlockSpec((2, size_z, blk, size_x), lambda i: (0, 0, i, 0)),
            pl.BlockSpec((size_z // 2, blk, size_x), lambda i: (0, i, 0)),
        ],
        out_specs=pl.BlockSpec((size_z, blk, size_x), lambda i: (0, i, 0)),
        out_shape=jax.ShapeDtypeStruct((size_z, size_y, size_x), f32),
        compiler_params=pltpu.CompilerParams(vmem_limit_bytes=40 * 2**20),
        cost_estimate=pl.CostEstimate(flops=10**10, bytes_accessed=5 * g.size, transcendentals=0),
    )(taps_z, g, expanded)


def z_halo_kernel(groups, w_ref, g_ref, p_ref, o_ref):
    def side(high):
        def body(r, carry):
            rows = pl.ds(pl.multiple_of(r * 8, 8), 8)
            acc = [p_ref[o, rows, :] for o in range(RADIUS)]
            for t in range(2):
                for z in range(RADIUS):
                    val = g_ref[t, z, rows, :]
                    for o in range(RADIUS):
                        off = z + RADIUS - o if high else z - RADIUS - o
                        if -RADIUS <= off <= RADIUS:
                            acc[o] = acc[o] + w_ref[t, off + RADIUS] * val
            for o in range(RADIUS):
                o_ref[o, rows, :] = acc[o]
            return carry

        lax.fori_loop(0, groups, body, 0)

    @pl.when(pl.program_id(0) == 0)
    def _():
        side(False)

    @pl.when(pl.program_id(0) == 1)
    def _():
        side(True)


def z_halo(taps_z, g_halo, partial):
    size_z, size_y, size_x = partial.shape
    blk = min(size_y, 128)
    last = size_z // RADIUS - 1
    spot = pl.BlockSpec((RADIUS, blk, size_x), lambda s, i: (s * last, i, 0))
    return pl.pallas_call(
        functools.partial(z_halo_kernel, blk // 8),
        grid=(2, size_y // blk),
        in_specs=[
            pl.BlockSpec(memory_space=pltpu.SMEM),
            pl.BlockSpec((2, RADIUS, blk, size_x), lambda s, i: (0, s, i, 0)),
            spot,
        ],
        out_specs=spot,
        out_shape=jax.ShapeDtypeStruct(partial.shape, f32),
        input_output_aliases={2: 0},
        compiler_params=pltpu.CompilerParams(vmem_limit_bytes=40 * 2**20),
    )(taps_z, g_halo, partial)


def pool_kernel(planes, c_ref, py_ref, px_ref, o_ref):
    for p in range(planes):
        both = c_ref[2 * p] + c_ref[2 * p + 1]
        high, low = split_in(both)
        along_x = mm(high, px_ref[...]) + mm(low, px_ref[...])
        high, low = split_in(along_x)
        o_ref[p] = mm(py_ref[...], high) + mm(py_ref[...], low)


def pool(block):
    size_z, size_y, size_x = block.shape
    planes = 4
    pick = lambda n, w: ((jnp.arange(n)[:, None] // 2 == jnp.arange(n // 2)[None, :]) * w).astype(bf16)
    px, py = pick(size_x, 0.5), pick(size_y, 0.25).T
    return pl.pallas_call(
        functools.partial(pool_kernel, planes),
        grid=(size_z // (2 * planes),),
        in_specs=[
            pl.BlockSpec((2 * planes, size_y, size_x), lambda i: (i, 0, 0)),
            pl.BlockSpec(py.shape, lambda i: (0, 0)),
            pl.BlockSpec(px.shape, lambda i: (0, 0)),
        ],
        out_specs=pl.BlockSpec((planes, size_y // 2, size_x // 2), lambda i: (i, 0, 0)),
        out_shape=jax.ShapeDtypeStruct((size_z // 2, size_y // 2, size_x // 2), f32),
    )(block, py, px)


def coarse_kernel(planes, w_ref, ext_ref, top_ref, bxh, bxl, byh, byl, o_ref):
    first = pl.program_id(0) * planes
    for p in range(planes):
        total = top_ref[0]
        sums = [0.0, 0.0]
        for k in range(2 * RADIUS + 1):
            val = ext_ref[first + p + k]
            for t in range(2):
                sums[t] = sums[t] + w_ref[t, k] * val
        for t in range(2):
            along_x = mm3(split_in(sums[t]), (bxh[t], bxl[t]))
            total = total + mm3((byh[t], byl[t]), split_in(along_x))
        o_ref[p] = total


def coarse_level(ext, taps, top_wide, size_z, size_y, size_x):
    planes = 2
    bx = split(band(taps[:, 0], size_x + 2 * RADIUS, size_x, 2))
    by = split(band(taps[:, 1], size_y + 2 * RADIUS, size_y, 2).transpose(0, 2, 1))
    mats = bx + by
    whole = lambda a: pl.BlockSpec(a.shape, lambda i: (0,) * a.ndim)
    return pl.pallas_call(
        functools.partial(coarse_kernel, planes),
        grid=(size_z // planes,),
        in_specs=[
            pl.BlockSpec(memory_space=pltpu.SMEM),
            whole(ext),
            pl.BlockSpec((1,) + top_wide.shape[1:], lambda i: (i * planes // TOPB, 0, 0)),
        ] + [whole(m) for m in mats],
        out_specs=pl.BlockSpec((planes, 2 * size_y, 2 * size_x), lambda i: (i, 0, 0)),
        out_shape=jax.ShapeDtypeStruct((size_z, 2 * size_y, 2 * size_x), f32),
        compiler_params=pltpu.CompilerParams(vmem_limit_bytes=40 * 2**20),
        cost_estimate=pl.CostEstimate(flops=10**10, bytes_accessed=10**7, transcendentals=0),
    )(taps[:, 2], ext, top_wide, *mats)


def coarse_halo(coarse):
    size_z, size_y, size_x = coarse.shape
    r = RADIUS
    face = (r, size_y * size_x // 128, 128)
    low = shift(coarse[-r:].reshape(face), "gz", 1).reshape(r, size_y, size_x)
    high = shift(coarse[:r].reshape(face), "gz", -1).reshape(r, size_y, size_x)
    ext = jnp.concatenate([low, coarse, high], axis=0)
    low = shift(ext[:, -r:], "gy", 1)
    high = shift(ext[:, :r], "gy", -1)
    ext = jnp.concatenate([low, ext, high], axis=1)
    low = shift(ext[:, :, -r:].transpose(0, 2, 1), "gx", 1).transpose(0, 2, 1)
    high = shift(ext[:, :, :r].transpose(0, 2, 1), "gx", -1).transpose(0, 2, 1)
    return jnp.concatenate([low, ext, high], axis=2)


def top_wide_field(coarse):
    size_z, size_y, size_x = coarse.shape
    nz, ny, nx = size_z // TOPB, size_y // TOPB, size_x // TOPB
    along_z = coarse.reshape(nz, TOPB, size_y, size_x).sum(axis=1)
    block_of = lambda n: (jnp.arange(n)[:, None] // TOPB == jnp.arange(n // TOPB)[None, :]).astype(f32)
    grid = jnp.einsum("zyx,yj,xi->zji", along_z, block_of(size_y), block_of(size_x), precision=precise)
    field = grid.reshape(1, nz * ny * nx)
    counts = []
    for axis in ("gx", "gy", "gz"):
        n = lax.axis_size(axis)
        counts.append(n)
        field = jnp.stack([field] + [shift(field, axis, s) for s in range(1, n)], axis=0)
        field = field.reshape(-1, nz * ny * nx)
    field = field.reshape(counts[2], counts[1], counts[0], nz, ny, nx)

    def apart(count, n):
        total = count * n
        place = -jnp.arange(count, dtype=jnp.int32)[:, None] * n + jnp.arange(n, dtype=jnp.int32)[None, :]
        dist = jnp.arange(n, dtype=jnp.int32)[:, None, None] - place[None]
        dist = dist % total
        near = jnp.minimum(dist, total - dist).astype(f32)
        return near * near

    dz, dy, dx = apart(counts[2], nz), apart(counts[1], ny), apart(counts[0], nx)
    square = (
        1.0
        + dz[:, None, None, :, None, None, :, None, None]
        + dy[None, :, None, None, :, None, None, :, None]
        + dx[None, None, :, None, None, :, None, None, :]
    )
    weights = (1.0 / (TOPB * TOPB * jnp.sqrt(square))).reshape(nz * ny * nx, -1)
    out = jnp.dot(weights, field.reshape(-1), precision=precise).reshape(nz, ny, nx)
    wide = lambda n: (jnp.arange(n)[:, None] == jnp.arange(n * TOPB * 2)[None, :] // (TOPB * 2)).astype(f32)
    return jnp.einsum("zyx,yj,xi->zji", out, wide(ny), wide(nx), precision=precise)


def sides(block):
    r = RADIUS
    ylo = shift(block[:, -r:], "gy", 1)
    yhi = shift(block[:, :r], "gy", -1)

    def turned(cols):
        strip = jnp.concatenate([ylo[:, :, cols], block[:, :, cols], yhi[:, :, cols]], axis=1)
        return strip.transpose(0, 2, 1)

    xlo = shift(turned(slice(-r, None)), "gx", 1)
    xhi = shift(turned(slice(0, r)), "gx", -1)
    return ylo, yhi, jnp.concatenate([xlo, xhi], axis=1)


def on_device(charges, fine_taps, coarse_taps):
    size_z, size_y, size_x = charges.shape
    r = RADIUS
    zlo = shift(charges[-r:], "gz", 1)
    zhi = shift(charges[:r], "gz", -1)

    band_x = band(fine_taps[:, 0], size_x + 2 * r, size_x)
    band_x = jnp.concatenate([band_x[0], band_x[1]], axis=1)
    edge_x = jnp.concatenate([band_x[:r], band_x[-r:]], axis=0)
    band_y = band(fine_taps[:, 1], size_y + 2 * r, size_y).transpose(0, 2, 1)
    mats = split(band_x[r:-r]) + split(edge_x) + split(band_y)
    taps_z = fine_taps[:, 2]

    g_own = xy_pass(charges, *sides(charges), mats)
    coarse = pool(charges)
    top_wide = top_wide_field(coarse)
    ext = coarse_halo(coarse)
    expanded = coarse_level(ext, coarse_taps, top_wide, *coarse.shape)
    partial = z_own(taps_z, g_own, expanded)

    halo = jnp.concatenate([zlo, zhi], axis=0)
    g_halo = xy_pass(halo, *sides(halo), mats)
    return z_halo(taps_z, g_halo, partial)


def solution(mesh):
    return jax.shard_map(
        on_device,
        mesh=mesh,
        in_specs=(P("gz", "gy", "gx"), P(), P()),
        out_specs=P("gz", "gy", "gx"),
        check_vma=False,
    )
```

```python
import functools

import jax
import jax.numpy as jnp
from jax import lax
from jax.experimental import pallas as pl
from jax.experimental.pallas import tpu as pltpu
from jax.sharding import PartitionSpec as P

RADIUS = 8
TOPB = 16
AXES = ("gz", "gy", "gx")
precise = lax.Precision.HIGHEST
f32, bf16 = jnp.float32, jnp.bfloat16


def shift(block, axis, by):
    n = lax.axis_size(axis)
    return lax.ppermute(block, axis, [(i, (i + by) % n) for i in range(n)])


def split(mat):
    high = lax.reduce_precision(mat, 8, 7)
    return high.astype(bf16), (mat - high).astype(bf16)


def split_in(val):
    high = val.astype(bf16)
    return high, (val - high.astype(f32)).astype(bf16)


def mm(a, b, dims=((1,), (0,))):
    return lax.dot_general(a, b, (dims, ((), ())), preferred_element_type=f32)


def mm3(a, b, dims=((1,), (0,))):
    return mm(a[0], b[0], dims) + mm(a[1], b[0], dims) + mm(a[0], b[1], dims)


def band(taps, length_in, length_out, repeat=1):
    spread = taps.shape[1]
    diff = (
        jnp.arange(length_in, dtype=jnp.int32)[:, None]
        - jnp.arange(length_out * repeat, dtype=jnp.int32)[None, :] // repeat
    )
    out = jnp.zeros((taps.shape[0],) + diff.shape, f32)
    for k in range(spread):
        out = jnp.where(diff[None] == k, taps[:, k, None, None], out)
    return out


def xy_kernel(planes, size_y, size_x, c_ref, ylo_ref, yhi_ref, xs_ref,
              bmh, bml, beh, bel, byh, byl, g_ref):
    ext_y = size_y + 2 * RADIUS
    rows = jnp.concatenate(
        [part for p in range(planes) for part in (ylo_ref[p], c_ref[p], yhi_ref[p])], axis=0
    )
    mid = mm3(split_in(rows), (bmh[...], bml[...]))
    parts = []
    for p in range(planes):
        edge = mm3(split_in(xs_ref[p]), (beh[...], bel[...]), ((0,), (0,)))
        parts.append(mid[p * ext_y:(p + 1) * ext_y] + edge)
    for t in range(2):
        right = jnp.concatenate([part[:, t * size_x:(t + 1) * size_x] for part in parts], axis=1)
        high, low = split_in(right)
        chunk, reach = byh.shape[1:]
        for y in range(0, size_y, chunk):
            out = mm3((byh[t], byl[t]), (high[y:y + reach], low[y:y + reach]))
            for p in range(planes):
                g_ref[t, p, y:y + chunk, :] = out[:, p * size_x:(p + 1) * size_x]


def xy_pass(block, ylo, yhi, xs, mats):
    size_z, size_y, size_x = block.shape
    planes = 4
    whole = lambda a: pl.BlockSpec(a.shape, lambda i: (0,) * a.ndim)
    lead = lambda a: pl.BlockSpec((planes,) + a.shape[1:], lambda i: (i, 0, 0))
    return pl.pallas_call(
        functools.partial(xy_kernel, planes, size_y, size_x),
        grid=(size_z // planes,),
        in_specs=[lead(a) for a in (block, ylo, yhi, xs)] + [whole(m) for m in mats],
        out_specs=pl.BlockSpec((2, planes, size_y, size_x), lambda i: (0, i, 0, 0)),
        out_shape=jax.ShapeDtypeStruct((2, size_z, size_y, size_x), f32),
        compiler_params=pltpu.CompilerParams(vmem_limit_bytes=40 * 2**20),
        cost_estimate=pl.CostEstimate(
            flops=size_z * 2 * 600 * 10**6 // 10, bytes_accessed=3 * block.size * 4, transcendentals=0
        ),
    )(block, ylo, yhi, xs, *mats)


def z_own_kernel(size_z, groups, w_ref, g_ref, e_ref, o_ref):
    def body(r, carry):
        rows = pl.ds(pl.multiple_of(r * 8, 8), 8)
        acc = [e_ref[o // 2, rows, :] for o in range(size_z)]
        for t in range(2):
            for z in range(size_z):
                val = g_ref[t, z, rows, :]
                for o in range(max(0, z - RADIUS), min(size_z, z + RADIUS + 1)):
                    acc[o] = acc[o] + w_ref[t, z - o + RADIUS] * val
        for o in range(size_z):
            o_ref[o, rows, :] = acc[o]
        return carry

    lax.fori_loop(0, groups, body, 0)


def z_own(taps_z, g, expanded):
    _, size_z, size_y, size_x = g.shape
    blk = 32
    return pl.pallas_call(
        functools.partial(z_own_kernel, size_z, blk // 8),
        grid=(size_y // blk,),
        in_specs=[
            pl.BlockSpec(memory_space=pltpu.SMEM),
            pl.BlockSpec((2, size_z, blk, size_x), lambda i: (0, 0, i, 0)),
            pl.BlockSpec((size_z // 2, blk, size_x), lambda i: (0, i, 0)),
        ],
        out_specs=pl.BlockSpec((size_z, blk, size_x), lambda i: (0, i, 0)),
        out_shape=jax.ShapeDtypeStruct((size_z, size_y, size_x), f32),
        compiler_params=pltpu.CompilerParams(vmem_limit_bytes=40 * 2**20),
        cost_estimate=pl.CostEstimate(flops=10**10, bytes_accessed=5 * g.size, transcendentals=0),
    )(taps_z, g, expanded)


def z_halo_kernel(groups, w_ref, g_ref, p_ref, o_ref):
    def side(high):
        def body(r, carry):
            rows = pl.ds(pl.multiple_of(r * 8, 8), 8)
            acc = [p_ref[o, rows, :] for o in range(RADIUS)]
            for t in range(2):
                for z in range(RADIUS):
                    val = g_ref[t, z, rows, :]
                    for o in range(RADIUS):
                        off = z + RADIUS - o if high else z - RADIUS - o
                        if -RADIUS <= off <= RADIUS:
                            acc[o] = acc[o] + w_ref[t, off + RADIUS] * val
            for o in range(RADIUS):
                o_ref[o, rows, :] = acc[o]
            return carry

        lax.fori_loop(0, groups, body, 0)

    @pl.when(pl.program_id(0) == 0)
    def _():
        side(False)

    @pl.when(pl.program_id(0) == 1)
    def _():
        side(True)


def z_halo(taps_z, g_halo, partial):
    size_z, size_y, size_x = partial.shape
    blk = min(size_y, 128)
    last = size_z // RADIUS - 1
    spot = pl.BlockSpec((RADIUS, blk, size_x), lambda s, i: (s * last, i, 0))
    return pl.pallas_call(
        functools.partial(z_halo_kernel, blk // 8),
        grid=(2, size_y // blk),
        in_specs=[
            pl.BlockSpec(memory_space=pltpu.SMEM),
            pl.BlockSpec((2, RADIUS, blk, size_x), lambda s, i: (0, s, i, 0)),
            spot,
        ],
        out_specs=spot,
        out_shape=jax.ShapeDtypeStruct(partial.shape, f32),
        input_output_aliases={2: 0},
        compiler_params=pltpu.CompilerParams(vmem_limit_bytes=40 * 2**20),
    )(taps_z, g_halo, partial)


def pool_kernel(planes, c_ref, py_ref, px_ref, o_ref):
    for p in range(planes):
        both = c_ref[2 * p] + c_ref[2 * p + 1]
        high, low = split_in(both)
        along_x = mm(high, px_ref[...]) + mm(low, px_ref[...])
        high, low = split_in(along_x)
        o_ref[p] = mm(py_ref[...], high) + mm(py_ref[...], low)


def pool(block):
    size_z, size_y, size_x = block.shape
    planes = 4
    pick = lambda n, w: ((jnp.arange(n)[:, None] // 2 == jnp.arange(n // 2)[None, :]) * w).astype(bf16)
    px, py = pick(size_x, 0.5), pick(size_y, 0.25).T
    return pl.pallas_call(
        functools.partial(pool_kernel, planes),
        grid=(size_z // (2 * planes),),
        in_specs=[
            pl.BlockSpec((2 * planes, size_y, size_x), lambda i: (i, 0, 0)),
            pl.BlockSpec(py.shape, lambda i: (0, 0)),
            pl.BlockSpec(px.shape, lambda i: (0, 0)),
        ],
        out_specs=pl.BlockSpec((planes, size_y // 2, size_x // 2), lambda i: (i, 0, 0)),
        out_shape=jax.ShapeDtypeStruct((size_z // 2, size_y // 2, size_x // 2), f32),
    )(block, py, px)


def coarse_kernel(planes, w_ref, ext_ref, top_ref, bxh, bxl, byh, byl, o_ref):
    first = pl.program_id(0) * planes
    for p in range(planes):
        total = top_ref[0]
        sums = [0.0, 0.0]
        for k in range(2 * RADIUS + 1):
            val = ext_ref[first + p + k]
            for t in range(2):
                sums[t] = sums[t] + w_ref[t, k] * val
        for t in range(2):
            along_x = mm3(split_in(sums[t]), (bxh[t], bxl[t]))
            total = total + mm3((byh[t], byl[t]), split_in(along_x))
        o_ref[p] = total


def coarse_level(ext, taps, top_wide, size_z, size_y, size_x):
    planes = 2
    bx = split(band(taps[:, 0], size_x + 2 * RADIUS, size_x, 2))
    by = split(band(taps[:, 1], size_y + 2 * RADIUS, size_y, 2).transpose(0, 2, 1))
    mats = bx + by
    whole = lambda a: pl.BlockSpec(a.shape, lambda i: (0,) * a.ndim)
    return pl.pallas_call(
        functools.partial(coarse_kernel, planes),
        grid=(size_z // planes,),
        in_specs=[
            pl.BlockSpec(memory_space=pltpu.SMEM),
            whole(ext),
            pl.BlockSpec((1,) + top_wide.shape[1:], lambda i: (i * planes // TOPB, 0, 0)),
        ] + [whole(m) for m in mats],
        out_specs=pl.BlockSpec((planes, 2 * size_y, 2 * size_x), lambda i: (i, 0, 0)),
        out_shape=jax.ShapeDtypeStruct((size_z, 2 * size_y, 2 * size_x), f32),
        compiler_params=pltpu.CompilerParams(vmem_limit_bytes=40 * 2**20),
        cost_estimate=pl.CostEstimate(flops=10**10, bytes_accessed=10**7, transcendentals=0),
    )(taps[:, 2], ext, top_wide, *mats)


def coarse_halo(coarse):
    size_z, size_y, size_x = coarse.shape
    r = RADIUS
    face = (r, size_y * size_x // 128, 128)
    low = shift(coarse[-r:].reshape(face), "gz", 1).reshape(r, size_y, size_x)
    high = shift(coarse[:r].reshape(face), "gz", -1).reshape(r, size_y, size_x)
    ext = jnp.concatenate([low, coarse, high], axis=0)
    low = shift(ext[:, -r:], "gy", 1)
    high = shift(ext[:, :r], "gy", -1)
    ext = jnp.concatenate([low, ext, high], axis=1)
    low = shift(ext[:, :, -r:].transpose(0, 2, 1), "gx", 1).transpose(0, 2, 1)
    high = shift(ext[:, :, :r].transpose(0, 2, 1), "gx", -1).transpose(0, 2, 1)
    return jnp.concatenate([low, ext, high], axis=2)


def top_wide_field(coarse):
    size_z, size_y, size_x = coarse.shape
    nz, ny, nx = size_z // TOPB, size_y // TOPB, size_x // TOPB
    along_z = coarse.reshape(nz, TOPB, size_y, size_x).sum(axis=1)
    block_of = lambda n: (jnp.arange(n)[:, None] // TOPB == jnp.arange(n // TOPB)[None, :]).astype(f32)
    grid = jnp.einsum("zyx,yj,xi->zji", along_z, block_of(size_y), block_of(size_x), precision=precise)
    field = grid.reshape(1, nz * ny * nx)
    counts = []
    for axis in ("gx", "gy", "gz"):
        n = lax.axis_size(axis)
        counts.append(n)
        field = jnp.stack([field] + [shift(field, axis, s) for s in range(1, n)], axis=0)
        field = field.reshape(-1, nz * ny * nx)
    field = field.reshape(counts[2], counts[1], counts[0], nz, ny, nx)

    def apart(count, n):
        total = count * n
        place = -jnp.arange(count, dtype=jnp.int32)[:, None] * n + jnp.arange(n, dtype=jnp.int32)[None, :]
        dist = jnp.arange(n, dtype=jnp.int32)[:, None, None] - place[None]
        dist = dist % total
        near = jnp.minimum(dist, total - dist).astype(f32)
        return near * near

    dz, dy, dx = apart(counts[2], nz), apart(counts[1], ny), apart(counts[0], nx)
    square = (
        1.0
        + dz[:, None, None, :, None, None, :, None, None]
        + dy[None, :, None, None, :, None, None, :, None]
        + dx[None, None, :, None, None, :, None, None, :]
    )
    weights = (1.0 / (TOPB * TOPB * jnp.sqrt(square))).reshape(nz * ny * nx, -1)
    out = jnp.dot(weights, field.reshape(-1), precision=precise).reshape(nz, ny, nx)
    wide = lambda n: (jnp.arange(n)[:, None] == jnp.arange(n * TOPB * 2)[None, :] // (TOPB * 2)).astype(f32)
    return jnp.einsum("zyx,yj,xi->zji", out, wide(ny), wide(nx), precision=precise)


def sides(block):
    r = RADIUS
    ylo = shift(block[:, -r:], "gy", 1)
    yhi = shift(block[:, :r], "gy", -1)

    def turned(cols):
        strip = jnp.concatenate([ylo[:, :, cols], block[:, :, cols], yhi[:, :, cols]], axis=1)
        return strip.transpose(0, 2, 1)

    xlo = shift(turned(slice(-r, None)), "gx", 1)
    xhi = shift(turned(slice(0, r)), "gx", -1)
    return ylo, yhi, jnp.concatenate([xlo, xhi], axis=1)


def on_device(charges, fine_taps, coarse_taps):
    size_z, size_y, size_x = charges.shape
    r = RADIUS
    zlo = shift(charges[-r:], "gz", 1)
    zhi = shift(charges[:r], "gz", -1)

    band_x = band(fine_taps[:, 0], size_x + 2 * r, size_x)
    band_x = jnp.concatenate([band_x[0], band_x[1]], axis=1)
    edge_x = jnp.concatenate([band_x[:r], band_x[-r:]], axis=0)
    chunk = 128 if size_y % 128 == 0 else size_y
    band_y = band(fine_taps[:, 1], chunk + 2 * r, chunk).transpose(0, 2, 1)
    mats = split(band_x[r:-r]) + split(edge_x) + split(band_y)
    taps_z = fine_taps[:, 2]

    g_own = xy_pass(charges, *sides(charges), mats)
    coarse = pool(charges)
    top_wide = top_wide_field(coarse)
    ext = coarse_halo(coarse)
    expanded = coarse_level(ext, coarse_taps, top_wide, *coarse.shape)
    partial = z_own(taps_z, g_own, expanded)

    halo = jnp.concatenate([zlo, zhi], axis=0)
    g_halo = xy_pass(halo, *sides(halo), mats)
    return z_halo(taps_z, g_halo, partial)


def solution(mesh):
    return jax.shard_map(
        on_device,
        mesh=mesh,
        in_specs=(P("gz", "gy", "gx"), P(), P()),
        out_specs=P("gz", "gy", "gx"),
        check_vma=False,
    )
```
